256 devices in a mesh: ctx: 32 (over z, y), chan: 8 (over x, core).
Axes of the slice: x: 4, y: 4, z: 8, core: 2. Of those that a mesh axis runs over, the one named last changes fastest.
Arguments:
- query_slab: bfloat16 [7168, 1024], P('ctx', 'chan'), may hold values from -6 to 6
- key_slab: bfloat16 [7168, 1024], P('ctx', 'chan'), may hold values from -6 to 6
- value_slab: bfloat16 [7168, 1024], P('ctx', 'chan'), may hold values from -6 to 6
- filters: float32 [7168, 1024], P('ctx', 'chan'), may hold values from -1.1 to 1.1, as said below
- out_weight: bfloat16 [1024, 8192], P(None, 'chan'), may hold values from -0.1875 to 0.1875
- grad_out: bfloat16 [7168, 8192], P('ctx', 'chan'), may hold values from -5 to 5
Outputs:
- layer_out: float32 [7168, 8192], P('ctx', 'chan')
- grad_query: float32 [7168, 1024], P('ctx', 'chan')
- grad_key: float32 [7168, 1024], P('ctx', 'chan')
- grad_value: float32 [7168, 1024], P('ctx', 'chan')
- grad_weight: float32 [1024, 8192], P('ctx', 'chan')
The draws below stay inside these ranges and needn't reach their ends.
Inputs may be any that keep to these rules, and one draw needn't show every extreme that they name: Real causal filters, one per channel.
All inputs are finite; a program needn't handle non-finite values.
Results may differ from the reference program's by a relative error of at most 0.0029.
Values may be sent and summed in bfloat16 or wider, within the bound.
No kernel may reach another device: no remote copies, remote signals or barrier semaphores. Data moves between devices by JAX's collectives and lax.ppermute only.
A program may use at most 64 MiB of HBM per device.

```python
import math
import jax
import jax.numpy as jnp

D = 8192
C = 1024
TOKENS = 7168


def unit_envelope(rate, positions):
    amplitude = jnp.sqrt((1.0 - jnp.exp(-2.0 * rate)) / (1.0 - jnp.exp(-2.0 * rate * TOKENS)))
    return amplitude * jnp.exp(-rate * positions)


def draw_filters(key, part):
    key = jax.random.fold_in(key, 17)
    key_mask, key_fast, key_slow, key_noise, key_share, key_tail = jax.random.split(key, 6)
    slow_share = 0.5
    slow_mask = jax.random.uniform(key_mask, (1, C)) < slow_share
    fast_rate = jax.random.uniform(key_fast, (1, C), minval=1.0 / 50.0, maxval=1.0 / 30.0)
    slow_rate = jnp.exp(jax.random.uniform(key_slow, (1, C), minval=math.log(0.05 / TOKENS), maxval=math.log(2.0 / TOKENS)))
    tail_rate = jnp.exp(jax.random.uniform(key_tail, (1, C), minval=math.log(0.05 / TOKENS), maxval=math.log(2.0 / TOKENS)))
    tail_share = jnp.exp(jax.random.uniform(key_share, (1, C), minval=math.log(0.005), maxval=math.log(0.3)))
    positions = jnp.arange(TOKENS, dtype=jnp.float32)[:, None]
    fast_envelope = jnp.sqrt(1.0 - tail_share) * unit_envelope(fast_rate, positions) + jnp.sqrt(tail_share) * unit_envelope(tail_rate, positions)
    slow_envelope = unit_envelope(slow_rate, positions)
    envelope = jnp.where(slow_mask, slow_envelope, fast_envelope)
    noise_draw = jnp.clip(jax.random.normal(key_noise, (TOKENS, C)), -3.9, 3.9)
    return jnp.clip(envelope * noise_draw, -1.1, 1.1).astype(jnp.float32)


def block_scale(rng, dims, shards, smallest, largest):
    loudness, own = 1.0, jax.random.fold_in(rng, 6)
    for position, shards_of in shards:
        heights = jnp.exp(jax.random.uniform(jax.random.fold_in(own, position), (shards_of,), jnp.float32, smallest / len(shards), largest / len(shards)))
        loudness = loudness * jnp.repeat(heights, dims[position] // shards_of).reshape([-1 if axis == position else 1 for axis in range(len(dims))])
    return loudness


def noise(rng, extent, scale, most, cuts=(), kind=jnp.bfloat16):
    result = scale * jax.random.normal(rng, extent, jnp.float32)
    if cuts:
        result = result * block_scale(rng, extent, cuts, -0.22, 0.18)
    return jnp.clip(result, -most, most).astype(kind)


def setup_inputs(seed: int = 0) -> dict:
    splits = jax.random.split(jax.random.key(seed), 7)
    return {
        "query_slab": noise(splits[0], (TOKENS, C), 1.0, 6.0, ((0, 32), (1, 8))),
        "key_slab": noise(splits[1], (TOKENS, C), 1.0, 6.0, ((0, 32), (1, 8))),
        "value_slab": noise(splits[2], (TOKENS, C), 1.0, 6.0, ((0, 32), (1, 8))),
        "filters": draw_filters(jax.random.fold_in(splits[6], 71), 0),
        "out_weight": noise(splits[4], (C, D), C ** -0.5, 0.1875, ((1, 8),)),
        "grad_out": noise(splits[5], (TOKENS, D), 0.35, 5.0, ((0, 32), (1, 8))),
    }


def causal_apply(signal, filt, adjoint):
    seq_length = signal.shape[0]
    signal_spec = jnp.fft.rfft(signal, n=2 * seq_length, axis=0)
    filter_spec = jnp.fft.rfft(filt, n=2 * seq_length, axis=0)
    if adjoint:
        filter_spec = jnp.conj(filter_spec)
    return jnp.fft.irfft(signal_spec * filter_spec, n=2 * seq_length, axis=0)[:seq_length]


def reference(query_slab, key_slab, value_slab, filters, out_weight, grad_out):
    query_f = query_slab.astype(jnp.float32)
    key_f = key_slab.astype(jnp.float32)
    value_f = value_slab.astype(jnp.float32)
    mixed_input = key_f * value_f
    conv_out = causal_apply(mixed_input, filters, False)
    gated_out = (query_f * conv_out).astype(jnp.bfloat16)
    layer_out = jnp.dot(gated_out, out_weight, preferred_element_type=jnp.float32)
    grad_gated = jnp.dot(grad_out, out_weight.T, preferred_element_type=jnp.float32)
    grad_query = grad_gated * conv_out
    grad_conv = grad_gated * query_f
    grad_mixed = causal_apply(grad_conv, filters, True)
    grad_key = grad_mixed * value_f
    grad_value = grad_mixed * key_f
    grad_weight = jnp.dot(gated_out.T, grad_out, preferred_element_type=jnp.float32)
    return (layer_out, grad_query, grad_key, grad_value, grad_weight)
```

```python
import jax
import jax.numpy as jnp
from jax import lax
from jax.experimental import pallas as pl
from jax.experimental.pallas import tpu as pltpu
from jax.sharding import PartitionSpec as P

VMEM_BYTES = 40 * 1024 * 1024


def partial_kernel(grad_ref, weight_ref, out_ref):
    for j in range(2):
        out_ref[j] = lax.dot_general(
            grad_ref[...],
            weight_ref[128 * j:128 * j + 128, :],
            (((1,), (1,)), ((), ())),
            preferred_element_type=jnp.float32,
        ).astype(jnp.bfloat16)


def partial_call(grad_out, out_weight):
    return pl.pallas_call(
        partial_kernel,
        out_shape=jax.ShapeDtypeStruct((8, 224, 128), jnp.bfloat16),
        grid=(4,),
        in_specs=[
            pl.BlockSpec((224, 1024), lambda i: (0, 0)),
            pl.BlockSpec((256, 1024), lambda i: (i, 0)),
        ],
        out_specs=pl.BlockSpec((2, 224, 128), lambda i: (i, 0, 0)),
        compiler_params=pltpu.CompilerParams(vmem_limit_bytes=VMEM_BYTES),
    )(grad_out, out_weight)


def pack_kernel(query_ref, key_ref, value_ref, filter_ref, partial_ref, send_ref, gated_ref):
    f32 = jnp.float32
    grad_gated = partial_ref[0].astype(f32)
    for j in range(1, 8):
        grad_gated = grad_gated + partial_ref[j].astype(f32)
    gated_ref[...] = grad_gated
    arrays = (
        key_ref[...].astype(f32) * value_ref[...].astype(f32),
        filter_ref[...],
        grad_gated * query_ref[...].astype(f32),
    )
    pad = jnp.zeros((16, 128), f32)
    for index, array in enumerate(arrays):
        for half in range(2):
            block = jnp.concatenate([array[112 * half:112 * half + 112], pad], axis=0).T
            for cc in range(4):
                row = (index * 2 + half) * 4 + cc
                send_ref[pl.ds(row, 32, stride=24), :] = block[32 * cc:32 * cc + 32]


def pack_call(query, key, value, filters, partials):
    return pl.pallas_call(
        pack_kernel,
        out_shape=(
            jax.ShapeDtypeStruct((768, 128), jnp.float32),
            jax.ShapeDtypeStruct((224, 128), jnp.float32),
        ),
        compiler_params=pltpu.CompilerParams(vmem_limit_bytes=VMEM_BYTES),
    )(query, key, value, filters, partials)


def conv_kernel(recv_ref, out_ref, xp, zp, fl, rh, rl, acc):
    f32, bf = jnp.float32, jnp.bfloat16
    row = lax.broadcasted_iota(jnp.int32, (16, 128), 0)
    lane = lax.broadcasted_iota(jnp.int32, (16, 128), 1)
    ri = lax.broadcasted_iota(jnp.int32, (64, 64), 0)
    ci = lax.broadcasted_iota(jnp.int32, (64, 64), 1)
    flip_blocks = jnp.where(ri + ci == 63, 1.0, 0.0).astype(bf)
    rows = lax.broadcasted_iota(jnp.int32, (128, 128), 0)
    cols = lax.broadcasted_iota(jnp.int32, (128, 128), 1)
    flip_lanes = jnp.where(rows + cols == 111, 1.0, 0.0).astype(bf)

    def split(block):
        high = block.astype(bf)
        return high, (block - high.astype(f32)).astype(bf)

    def flip(block):
        pair = jnp.concatenate(split(block), axis=0)
        turned = jnp.dot(pair, flip_lanes, preferred_element_type=f32).astype(bf)
        pair = jnp.concatenate([turned[0:64], turned[64:128]], axis=1)
        turned = jnp.dot(flip_blocks, pair, preferred_element_type=f32)
        return turned[:, 0:128] + turned[:, 128:256]

    xp[0:64, :] = jnp.zeros((64, 128), f32)
    zp[0:64, :] = jnp.zeros((64, 128), f32)
    for m in range(8):
        rh[128 * m + 112:128 * m + 128, :] = jnp.zeros((16, 1024), bf)
        rl[128 * m + 112:128 * m + 128, :] = jnp.zeros((16, 1024), bf)
    for d in range(2):
        acc[d, 0:8, :] = jnp.zeros((8, 1024), f32)
    fl[0:8, :] = jnp.zeros((8, 128), f32)

    for cc in range(4):
        for half in range(2):
            xp[pl.ds(64 + half, 32, stride=2), :] = recv_ref[pl.ds(half * 4 + cc, 32, stride=24), :]
            fl[pl.ds(8 + half, 32, stride=2), :] = recv_ref[pl.ds(8 + half * 4 + cc, 32, stride=24), :]
            zp[pl.ds(64 + half, 32, stride=2), :] = recv_ref[pl.ds(16 + half * 4 + cc, 32, stride=24), :]
        zp[64:128, :] = flip(zp[64:128, :])
        for k in range(64):
            m, r = k // 8, k % 8
            left = jnp.broadcast_to(fl[8 + k:9 + k, :], (16, 128))
            right = jnp.broadcast_to(pltpu.roll(fl[7 + k:8 + k, :], 16, 1), (16, 128))
            for p in range(7):
                src = jnp.where(lane < 128 - 16 * p - row, left, right)
                rolled = pltpu.roll(src, 16 * p, 1, stride=1, stride_axis=0)
                high, low = split(rolled)
                rh[128 * m + 16 * p:128 * m + 16 * p + 16, 128 * r:128 * r + 128] = high
                rl[128 * m + 16 * p:128 * m + 16 * p + 16, 128 * r:128 * r + 128] = low
        lhs = jnp.concatenate(
            [
                jnp.concatenate([ref[64 - 8 * m:128 - 8 * m, :] for m in range(8)], axis=1)
                for ref in (xp, zp)
            ],
            axis=0,
        )
        lhs_high, lhs_low = split(lhs)
        prod = (
            jnp.dot(lhs_high, rh[...], preferred_element_type=f32)
            + jnp.dot(lhs_low, rh[...], preferred_element_type=f32)
            + jnp.dot(lhs_high, rl[...], preferred_element_type=f32)
        )
        acc[0, 8:72, :] = prod[0:64]
        acc[1, 8:72, :] = prod[64:128]
        for d in range(2):
            total = acc[d, 8:72, 0:128]
            for r in range(1, 8):
                total = total + acc[d, 8 - r:72 - r, 128 * r:128 * r + 128]
            if d == 1:
                total = flip(total)
            xp[64:128, :] = total
            for half in range(2):
                out_ref[pl.ds((d * 2 + half) * 4 + cc, 32, stride=16), :] = xp[pl.ds(64 + half, 32, stride=2), :]

def conv_call(recv):
    f32, bf = jnp.float32, jnp.bfloat16
    return pl.pallas_call(
        conv_kernel,
        out_shape=jax.ShapeDtypeStruct((512, 128), f32),
        in_specs=[pl.BlockSpec(memory_space=pltpu.VMEM)],
        out_specs=pl.BlockSpec(memory_space=pltpu.VMEM),
        scratch_shapes=[
            pltpu.VMEM((128, 128), f32),
            pltpu.VMEM((128, 128), f32),
            pltpu.VMEM((72, 128), f32),
            pltpu.VMEM((1024, 1024), bf),
            pltpu.VMEM((1024, 1024), bf),
            pltpu.VMEM((2, 72, 1024), f32),
        ],
        compiler_params=pltpu.CompilerParams(vmem_limit_bytes=32 * 1024 * 1024),
    )(recv)


def unpack_kernel(recv_ref, query_ref, key_ref, value_ref, grad_ref, gated_ref, gq_ref, gk_ref, gv_ref):
    f32 = jnp.float32
    for half in range(2):
        rows = slice(112 * half, 112 * half + 112)
        blocks = []
        for index in range(2):
            pieces = [recv_ref[pl.ds((index * 2 + half) * 4 + cc, 32, stride=16), :] for cc in range(4)]
            blocks.append(jnp.concatenate(pieces, axis=0).T[0:112])
        conv_out, grad_mixed = blocks
        gated_ref[rows, :] = (query_ref[rows, :].astype(f32) * conv_out).astype(jnp.bfloat16)
        gq_ref[rows, :] = grad_ref[rows, :] * conv_out
        gk_ref[rows, :] = grad_mixed * value_ref[rows, :].astype(f32)
        gv_ref[rows, :] = grad_mixed * key_ref[rows, :].astype(f32)


def unpack_call(recv, query, key, value, grad_gated):
    grad = jax.ShapeDtypeStruct((224, 128), jnp.float32)
    return pl.pallas_call(
        unpack_kernel,
        out_shape=(jax.ShapeDtypeStruct((224, 128), jnp.bfloat16), grad, grad, grad),
        compiler_params=pltpu.CompilerParams(vmem_limit_bytes=VMEM_BYTES),
    )(recv, query, key, value, grad_gated)


def weight_kernel(gated_ref, grad_ref, out_ref, total):
    step = pl.program_id(0)
    part = lax.dot_general(
        gated_ref[0, 0], grad_ref[0], (((0,), (0,)), ((), ())), preferred_element_type=jnp.float32
    )

    @pl.when(step == 0)
    def _():
        total[...] = part

    @pl.when(step > 0)
    def _():
        total[...] += part

    @pl.when(step == 7)
    def _():
        out_ref[...] = total[...].astype(jnp.bfloat16)


def weight_call(gathered, grad_planes):
    return pl.pallas_call(
        weight_kernel,
        out_shape=jax.ShapeDtypeStruct((128, 1024), jnp.bfloat16),
        grid=(8,),
        in_specs=[
            pl.BlockSpec((1, 1, 224, 128), lambda i: (i, 1, 0, 0)),
            pl.BlockSpec((1, 224, 1024), lambda i: (i, 0, 0)),
        ],
        out_specs=pl.BlockSpec((128, 1024), lambda i: (0, 0)),
        scratch_shapes=[pltpu.VMEM((128, 1024), jnp.float32)],
        compiler_params=pltpu.CompilerParams(vmem_limit_bytes=VMEM_BYTES),
    )(gathered, grad_planes)


def layer_kernel(gated_ref, weight_ref, out_ref):
    full = jnp.concatenate([gated_ref[j, 0] for j in range(8)], axis=1)
    out_ref[...] = jnp.dot(full, weight_ref[...], preferred_element_type=jnp.float32)


def layer_call(gathered, out_weight):
    return pl.pallas_call(
        layer_kernel,
        out_shape=jax.ShapeDtypeStruct((224, 1024), jnp.float32),
        grid=(4,),
        in_specs=[
            pl.BlockSpec((8, 1, 224, 128), lambda i: (0, 0, 0, 0)),
            pl.BlockSpec((1024, 256), lambda i: (0, i)),
        ],
        out_specs=pl.BlockSpec((224, 256), lambda i: (0, i)),
        compiler_params=pltpu.CompilerParams(vmem_limit_bytes=VMEM_BYTES),
    )(gathered, out_weight)


def local(query_slab, key_slab, value_slab, filters, out_weight, grad_out):
    along_z = [[4 * z + y for z in range(8)] for y in range(4)]
    swap = [
        ((z * 4 + y) * 8 + j, (j * 4 + y) * 8 + z)
        for z in range(8)
        for y in range(4)
        for j in range(8)
    ]
    own_y = lax.axis_index("ctx") % 4
    grad_planes = lax.all_gather(grad_out, "ctx", axis=0, axis_index_groups=along_z)
    partials = partial_call(grad_out, out_weight)
    partials = lax.all_to_all(partials, "chan", 0, 0)
    sent, grad_gated = pack_call(query_slab, key_slab, value_slab, filters, partials)
    by_channel = lax.all_to_all(sent.reshape(32, 24, 128), "ctx", 0, 0).reshape(768, 128)
    convolved = conv_call(by_channel)
    by_token = lax.all_to_all(convolved.reshape(32, 16, 128), "ctx", 0, 0).reshape(512, 128)
    gated, grad_query, grad_key, grad_value = unpack_call(
        by_token, query_slab, key_slab, value_slab, grad_gated
    )
    swapped = lax.ppermute(gated, ("ctx", "chan"), swap)
    gathered = lax.all_gather(jnp.stack([gated, swapped]), "chan", axis=0)
    weight_part = weight_call(gathered, grad_planes).reshape(4, 32, 1024)
    total = lax.dynamic_index_in_dim(weight_part, own_y, 0, keepdims=False).astype(jnp.float32)
    arrived = []
    for step in range(1, 4):
        block = lax.dynamic_index_in_dim(weight_part, own_y ^ step, 0, keepdims=False)
        arrived.append(lax.ppermute(block, "ctx", [(i, i ^ step) for i in range(32)]))
    layer_out = layer_call(gathered, out_weight)
    for block in arrived:
        total = total + block.astype(jnp.float32)
    return (layer_out, grad_query, grad_key, grad_value, total)


def solution(mesh):
    placed = (
        P("ctx", "chan"),
        P("ctx", "chan"),
        P("ctx", "chan"),
        P("ctx", "chan"),
        P(None, "chan"),
        P("ctx", "chan"),
    )
    return jax.shard_map(
        local,
        mesh=mesh,
        in_specs=placed,
        out_specs=(
            P("ctx", "chan"),
            P("ctx", "chan"),
            P("ctx", "chan"),
            P("ctx", "chan"),
            P("ctx", "chan"),
        ),
        check_vma=False,
    )
```

```python
import jax
import jax.numpy as jnp
from jax import lax
from jax.experimental import pallas as pl
from jax.experimental.pallas import tpu as pltpu
from jax.sharding import PartitionSpec as P

VMEM_BYTES = 16 * 1024 * 1024
WHOLE_BYTES = 60 * 1024 * 1024


def partial_kernel(
    grad_hbm, weight_hbm, out_hbm, grad_ref, weight_ref, out_ref, grad_sem, weight_sem, out_sem
):
    def grad_copy(part):
        rows = pl.ds(112 * part, 112)
        return pltpu.make_async_copy(grad_hbm.at[rows], grad_ref.at[rows], grad_sem.at[part])

    def weight_copy(part):
        rows = pl.ds(128 * part, 128)
        return pltpu.make_async_copy(weight_hbm.at[rows], weight_ref.at[rows], weight_sem.at[part])

    for part in range(2):
        grad_copy(part).start()
    for part in range(8):
        weight_copy(part).start()
    for part in range(2):
        grad_copy(part).wait()
    out_copies = []
    for j in range(0, 8, 2):
        weight_copy(j).wait()
        weight_copy(j + 1).wait()
        product = lax.dot_general(
            grad_ref[...],
            weight_ref[128 * j:128 * j + 256, :],
            (((1,), (1,)), ((), ())),
            preferred_element_type=jnp.float32,
        ).astype(jnp.bfloat16)
        out_ref[j] = product[:, 0:128]
        out_ref[j + 1] = product[:, 128:256]
        out_copies.append(
            pltpu.make_async_copy(
                out_ref.at[pl.ds(j, 2)], out_hbm.at[pl.ds(j, 2)], out_sem.at[j // 2]
            )
        )
        out_copies[-1].start()
    for copy in out_copies:
        copy.wait()


def partial_call(grad_out, out_weight):
    return pl.pallas_call(
        partial_kernel,
        out_shape=jax.ShapeDtypeStruct((8, 224, 128), jnp.bfloat16),
        in_specs=[
            pl.BlockSpec(memory_space=pltpu.MemorySpace.HBM),
            pl.BlockSpec(memory_space=pltpu.MemorySpace.HBM),
        ],
        out_specs=pl.BlockSpec(memory_space=pltpu.MemorySpace.HBM),
        scratch_shapes=[
            pltpu.VMEM((224, 1024), jnp.bfloat16),
            pltpu.VMEM((1024, 1024), jnp.bfloat16),
            pltpu.VMEM((8, 224, 128), jnp.bfloat16),
            pltpu.SemaphoreType.DMA((2,)),
            pltpu.SemaphoreType.DMA((8,)),
            pltpu.SemaphoreType.DMA((4,)),
        ],
        compiler_params=pltpu.CompilerParams(vmem_limit_bytes=WHOLE_BYTES),
    )(grad_out, out_weight)


def pack_kernel(query_ref, key_ref, value_ref, filter_ref, partial_ref, send_ref, gated_ref):
    f32 = jnp.float32
    grad_gated = partial_ref[0].astype(f32)
    for j in range(1, 8):
        grad_gated = grad_gated + partial_ref[j].astype(f32)
    gated_ref[...] = grad_gated
    arrays = (
        key_ref[...].astype(f32) * value_ref[...].astype(f32),
        filter_ref[...],
        grad_gated * query_ref[...].astype(f32),
    )
    pad = jnp.zeros((16, 128), f32)
    for index, array in enumerate(arrays):
        for half in range(2):
            block = jnp.concatenate([array[112 * half:112 * half + 112], pad], axis=0).T
            for cc in range(4):
                row = (index * 2 + half) * 4 + cc
                send_ref[pl.ds(row, 32, stride=24), :] = block[32 * cc:32 * cc + 32]


def pack_call(query, key, value, filters, partials):
    return pl.pallas_call(
        pack_kernel,
        out_shape=(
            jax.ShapeDtypeStruct((768, 128), jnp.float32),
            jax.ShapeDtypeStruct((224, 128), jnp.float32),
        ),
        compiler_params=pltpu.CompilerParams(vmem_limit_bytes=VMEM_BYTES),
    )(query, key, value, filters, partials)


def conv_kernel(recv_ref, out_ref, xp, zp, fl, rh, rl, acc):
    f32, bf = jnp.float32, jnp.bfloat16
    row = lax.broadcasted_iota(jnp.int32, (16, 128), 0)
    lane = lax.broadcasted_iota(jnp.int32, (16, 128), 1)
    ri = lax.broadcasted_iota(jnp.int32, (64, 64), 0)
    ci = lax.broadcasted_iota(jnp.int32, (64, 64), 1)
    flip_blocks = jnp.where(ri + ci == 63, 1.0, 0.0).astype(bf)
    rows = lax.broadcasted_iota(jnp.int32, (128, 128), 0)
    cols = lax.broadcasted_iota(jnp.int32, (128, 128), 1)
    flip_lanes = jnp.where(rows + cols == 111, 1.0, 0.0).astype(bf)

    def split(block):
        high = block.astype(bf)
        return high, (block - high.astype(f32)).astype(bf)

    def flip(block):
        pair = jnp.concatenate(split(block), axis=0)
        turned = jnp.dot(pair, flip_lanes, preferred_element_type=f32).astype(bf)
        pair = jnp.concatenate([turned[0:64], turned[64:128]], axis=1)
        turned = jnp.dot(flip_blocks, pair, preferred_element_type=f32)
        return turned[:, 0:128] + turned[:, 128:256]

    xp[0:64, :] = jnp.zeros((64, 128), f32)
    zp[0:64, :] = jnp.zeros((64, 128), f32)
    for m in range(8):
        rh[128 * m + 112:128 * m + 128, :] = jnp.zeros((16, 1024), bf)
        rl[128 * m + 112:128 * m + 128, :] = jnp.zeros((16, 1024), bf)
    for d in range(2):
        acc[d, 0:8, :] = jnp.zeros((8, 1024), f32)
    fl[0:8, :] = jnp.zeros((8, 128), f32)

    for cc in range(4):
        for half in range(2):
            xp[pl.ds(64 + half, 32, stride=2), :] = recv_ref[pl.ds(half * 4 + cc, 32, stride=24), :]
            fl[pl.ds(8 + half, 32, stride=2), :] = recv_ref[pl.ds(8 + half * 4 + cc, 32, stride=24), :]
            zp[pl.ds(64 + half, 32, stride=2), :] = recv_ref[pl.ds(16 + half * 4 + cc, 32, stride=24), :]
        zp[64:128, :] = flip(zp[64:128, :])
        for k in range(64):
            m, r = k // 8, k % 8
            left = jnp.broadcast_to(fl[8 + k:9 + k, :], (16, 128))
            right = jnp.broadcast_to(pltpu.roll(fl[7 + k:8 + k, :], 16, 1), (16, 128))
            for p in range(7):
                src = jnp.where(lane < 128 - 16 * p - row, left, right)
                rolled = pltpu.roll(src, 16 * p, 1, stride=1, stride_axis=0)
                high, low = split(rolled)
                rh[128 * m + 16 * p:128 * m + 16 * p + 16, 128 * r:128 * r + 128] = high
                rl[128 * m + 16 * p:128 * m + 16 * p + 16, 128 * r:128 * r + 128] = low
        lhs = jnp.concatenate(
            [
                jnp.concatenate([ref[64 - 8 * m:128 - 8 * m, :] for m in range(8)], axis=1)
                for ref in (xp, zp)
            ],
            axis=0,
        )
        lhs_high, lhs_low = split(lhs)
        for n in range(0, 1024, 256):
            cols = slice(n, n + 256)
            prod = (
                jnp.dot(lhs_high, rh[:, cols], preferred_element_type=f32)
                + jnp.dot(lhs_low, rh[:, cols], preferred_element_type=f32)
                + jnp.dot(lhs_high, rl[:, cols], preferred_element_type=f32)
            )
            acc[0, 8:72, cols] = prod[0:64]
            acc[1, 8:72, cols] = prod[64:128]
        for d in range(2):
            total = acc[d, 8:72, 0:128]
            for r in range(1, 8):
                total = total + acc[d, 8 - r:72 - r, 128 * r:128 * r + 128]
            if d == 1:
                total = flip(total)
            xp[64:128, :] = total
            for half in range(2):
                out_ref[pl.ds((d * 2 + half) * 4 + cc, 32, stride=16), :] = xp[pl.ds(64 + half, 32, stride=2), :]

def conv_call(recv):
    f32, bf = jnp.float32, jnp.bfloat16
    return pl.pallas_call(
        conv_kernel,
        out_shape=jax.ShapeDtypeStruct((512, 128), f32),
        in_specs=[pl.BlockSpec(memory_space=pltpu.VMEM)],
        out_specs=pl.BlockSpec(memory_space=pltpu.VMEM),
        scratch_shapes=[
            pltpu.VMEM((128, 128), f32),
            pltpu.VMEM((128, 128), f32),
            pltpu.VMEM((72, 128), f32),
            pltpu.VMEM((1024, 1024), bf),
            pltpu.VMEM((1024, 1024), bf),
            pltpu.VMEM((2, 72, 1024), f32),
        ],
        compiler_params=pltpu.CompilerParams(vmem_limit_bytes=VMEM_BYTES),
    )(recv)


def unpack_kernel(
    recv_ref, query_ref, key_ref, value_ref, grad_ref, send_ref, gated_hbm, gq_ref, gk_ref, gv_ref,
    gated_ref, sem,
):
    f32 = jnp.float32
    pad = jnp.zeros((16, 128), f32)
    gated_copies = []
    for half in range(2):
        rows = slice(112 * half, 112 * half + 112)
        blocks = []
        for index in range(2):
            pieces = [recv_ref[pl.ds((index * 2 + half) * 4 + cc, 32, stride=16), :] for cc in range(4)]
            blocks.append(jnp.concatenate(pieces, axis=0))
        conv_out = blocks[0].T[0:112]
        grad_mixed = blocks[1].T[0:112]
        query = query_ref[rows, :].astype(f32)
        by_channel = jnp.concatenate([query, pad], axis=0).T * blocks[0]
        by_channel = by_channel.astype(jnp.bfloat16)
        for y in range(4):
            for j in range(8):
                send_ref[8 * y + j, 32 * half:32 * half + 32, :] = by_channel[32 * y:32 * y + 32]
        gated_ref[rows, :] = (query * conv_out).astype(jnp.bfloat16)
        gq_ref[rows, :] = grad_ref[rows, :] * conv_out
        gated_copy = pltpu.make_async_copy(
            gated_ref.at[pl.ds(112 * half, 112)], gated_hbm.at[pl.ds(112 * half, 112)], sem.at[half]
        )
        gated_copy.start()
        gated_copies.append(gated_copy)
        gk_ref[rows, :] = grad_mixed * value_ref[rows, :].astype(f32)
        gv_ref[rows, :] = grad_mixed * key_ref[rows, :].astype(f32)
    for gated_copy in gated_copies:
        gated_copy.wait()


def unpack_call(recv, query, key, value, grad_gated):
    bf = jnp.bfloat16
    grad = jax.ShapeDtypeStruct((224, 128), jnp.float32)
    return pl.pallas_call(
        unpack_kernel,
        out_shape=(
            jax.ShapeDtypeStruct((32, 64, 128), bf),
            jax.ShapeDtypeStruct((224, 128), bf),
            grad,
            grad,
            grad,
        ),
        out_specs=tuple(
            pl.BlockSpec(memory_space=pltpu.MemorySpace.HBM if index == 1 else pltpu.VMEM)
            for index in range(5)
        ),
        scratch_shapes=[
            pltpu.VMEM((224, 128), bf),
            pltpu.SemaphoreType.DMA((2,)),
        ],
        compiler_params=pltpu.CompilerParams(vmem_limit_bytes=VMEM_BYTES),
    )(recv, query, key, value, grad_gated)


def weight_kernel(
    own_ref, gated_hbm, own, before, after, far_low, far_high, out_hbm,
    gated_ref, rows_ref, out_ref, gated_sem, sem, out_sem,
):
    parts = (
        (own, 0),
        (own, 112),
        (after, 0),
        (after, 112),
        (far_low, 0),
        (far_high, 0),
        (before, 0),
        (before, 112),
    )
    gated_copies, copies = [], []
    for turn in range(4):
        source = lax.rem(own_ref[0] + turn, 4)
        gated_copies.append(
            pltpu.make_async_copy(
                gated_hbm.at[pl.ds(8 * source, 8)], gated_ref.at[turn], gated_sem.at[turn]
            )
        )
        gated_copies[-1].start()
        for index in (2 * turn, 2 * turn + 1):
            source, start = parts[index]
            copies.append(
                pltpu.make_async_copy(
                    source.at[pl.ds(start, 112)],
                    rows_ref.at[pl.ds(128 * index, 112)],
                    sem.at[index],
                )
            )
            copies[-1].start()
    for index in range(8):
        rows_ref[128 * index + 112:128 * index + 128, :] = jnp.zeros((16, 1024), jnp.bfloat16)
    lhs = []
    for turn in range(4):
        gated_copies[turn].wait()
        copies[2 * turn].wait()
        copies[2 * turn + 1].wait()
        block = gated_ref[turn]
        lhs.append(block[:, 0:32, :].reshape(256, 128))
        lhs.append(block[:, 32:64, :].reshape(256, 128))
    lhs = jnp.concatenate(lhs, axis=1)
    out_copies = []
    for n in range(4):
        cols = pl.ds(256 * n, 256)
        out_ref[:, 256 * n:256 * n + 256] = jnp.dot(
            lhs, rows_ref[:, 256 * n:256 * n + 256], preferred_element_type=jnp.float32
        ).astype(jnp.bfloat16)
        out_copies.append(
            pltpu.make_async_copy(out_ref.at[:, cols], out_hbm.at[:, cols], out_sem.at[n])
        )
        out_copies[-1].start()
    for copy in out_copies:
        copy.wait()


def weight_call(own_y, gathered, parts):
    hbm = pl.BlockSpec(memory_space=pltpu.MemorySpace.HBM)
    return pl.pallas_call(
        weight_kernel,
        out_shape=jax.ShapeDtypeStruct((256, 1024), jnp.bfloat16),
        in_specs=[pl.BlockSpec(memory_space=pltpu.SMEM)] + [hbm] * 6,
        out_specs=hbm,
        scratch_shapes=[
            pltpu.VMEM((4, 8, 64, 128), jnp.bfloat16),
            pltpu.VMEM((1024, 1024), jnp.bfloat16),
            pltpu.VMEM((256, 1024), jnp.bfloat16),
            pltpu.SemaphoreType.DMA((4,)),
            pltpu.SemaphoreType.DMA((8,)),
            pltpu.SemaphoreType.DMA((4,)),
        ],
        compiler_params=pltpu.CompilerParams(vmem_limit_bytes=WHOLE_BYTES),
        cost_estimate=pl.CostEstimate(
            flops=2 * 256 * 896 * 1024, bytes_accessed=3 * 1024 * 1024, transcendentals=0
        ),
    )(own_y, gathered, *parts)


def layer_kernel(gated_ref, weight_ref, out_ref):
    full = jnp.concatenate([gated_ref[j] for j in range(8)], axis=1)
    out_ref[...] = jnp.dot(full, weight_ref[...], preferred_element_type=jnp.float32)


def layer_call(gathered, out_weight):
    return pl.pallas_call(
        layer_kernel,
        out_shape=jax.ShapeDtypeStruct((224, 1024), jnp.float32),
        grid=(4,),
        in_specs=[
            pl.BlockSpec((8, 224, 128), lambda i: (0, 0, 0)),
            pl.BlockSpec((1024, 256), lambda i: (0, i)),
        ],
        out_specs=pl.BlockSpec((224, 256), lambda i: (0, i)),
        compiler_params=pltpu.CompilerParams(vmem_limit_bytes=VMEM_BYTES),
    )(gathered, out_weight)


def local(query_slab, key_slab, value_slab, filters, out_weight, grad_out):
    up = [(4 * z + y, 4 * z + (y + 1) % 4) for z in range(8) for y in range(4)]
    down = [(4 * z + y, 4 * z + (y + 3) % 4) for z in range(8) for y in range(4)]
    along_z = [[4 * z + y for z in range(8)] for y in range(4)]
    planes = [list(range(32 * z, 32 * z + 32)) for z in range(8)]
    together = lax.optimization_barrier
    own_y = (lax.axis_index("ctx") % 4).astype(jnp.int32).reshape(1)
    before = lax.ppermute(grad_out, "ctx", up)
    after = lax.ppermute(grad_out, "ctx", down)
    partials = partial_call(grad_out, out_weight)
    partials = lax.all_to_all(partials, "chan", 0, 0)
    before, after, own_y, partials = together((before, after, own_y, partials))
    sent, grad_gated = pack_call(query_slab, key_slab, value_slab, filters, partials)
    by_channel = lax.all_to_all(sent.reshape(32, 24, 128), "ctx", 0, 0).reshape(768, 128)
    before, after, by_channel = together((before, after, by_channel))
    far_low = lax.ppermute(after[0:112], "ctx", down)
    far_high = lax.ppermute(before[112:224], "ctx", up)
    convolved = conv_call(by_channel)
    far_low, far_high, convolved = together((far_low, far_high, convolved))
    by_token = lax.all_to_all(convolved.reshape(32, 16, 128), "ctx", 0, 0).reshape(512, 128)
    plane_sent, gated, grad_query, grad_key, grad_value = unpack_call(
        by_token, query_slab, key_slab, value_slab, grad_gated
    )
    plane_gated = lax.all_to_all(plane_sent, ("ctx", "chan"), 0, 0, axis_index_groups=planes)
    weight_part = weight_call(
        own_y, plane_gated, (grad_out, before, after, far_low, far_high)
    ).reshape(8, 32, 1024)
    arrived = lax.all_to_all(weight_part, "ctx", 0, 0, axis_index_groups=along_z)
    full_gated = lax.all_gather(gated, "chan", axis=0)
    layer_out = layer_call(full_gated, out_weight)
    grad_weight = jnp.sum(arrived.astype(jnp.float32), axis=0)
    return (layer_out, grad_query, grad_key, grad_value, grad_weight)


def solution(mesh):
    placed = (
        P("ctx", "chan"),
        P("ctx", "chan"),
        P("ctx", "chan"),
        P("ctx", "chan"),
        P(None, "chan"),
        P("ctx", "chan"),
    )
    return jax.shard_map(
        local,
        mesh=mesh,
        in_specs=placed,
        out_specs=(
            P("ctx", "chan"),
            P("ctx", "chan"),
            P("ctx", "chan"),
            P("ctx", "chan"),
            P("ctx", "chan"),
        ),
        check_vma=False,
    )
```

```python
import jax
import jax.numpy as jnp
from jax import lax
from jax.experimental import pallas as pl
from jax.experimental.pallas import tpu as pltpu
from jax.sharding import PartitionSpec as P

VMEM_BYTES = 16 * 1024 * 1024
WHOLE_BYTES = 60 * 1024 * 1024


def partial_kernel(
    grad_hbm, weight_hbm, out_hbm, grad_ref, weight_ref, out_ref, grad_sem, weight_sem, out_sem
):
    def grad_copy(part):
        rows = pl.ds(112 * part, 112)
        return pltpu.make_async_copy(grad_hbm.at[rows], grad_ref.at[rows], grad_sem.at[part])

    def weight_copy(part):
        rows = pl.ds(128 * part, 128)
        return pltpu.make_async_copy(weight_hbm.at[rows], weight_ref.at[rows], weight_sem.at[part])

    for part in range(2):
        grad_copy(part).start()
    for part in range(8):
        weight_copy(part).start()
    for part in range(2):
        grad_copy(part).wait()
    out_copies = []
    for j in range(0, 8, 2):
        weight_copy(j).wait()
        weight_copy(j + 1).wait()
        product = lax.dot_general(
            grad_ref[...],
            weight_ref[128 * j:128 * j + 256, :],
            (((1,), (1,)), ((), ())),
            preferred_element_type=jnp.float32,
        ).astype(jnp.bfloat16)
        out_ref[j] = product[:, 0:128]
        out_ref[j + 1] = product[:, 128:256]
        out_copies.append(
            pltpu.make_async_copy(
                out_ref.at[pl.ds(j, 2)], out_hbm.at[pl.ds(j, 2)], out_sem.at[j // 2]
            )
        )
        out_copies[-1].start()
    for copy in out_copies:
        copy.wait()


def partial_call(grad_out, out_weight):
    return pl.pallas_call(
        partial_kernel,
        out_shape=jax.ShapeDtypeStruct((8, 224, 128), jnp.bfloat16),
        in_specs=[
            pl.BlockSpec(memory_space=pltpu.MemorySpace.HBM),
            pl.BlockSpec(memory_space=pltpu.MemorySpace.HBM),
        ],
        out_specs=pl.BlockSpec(memory_space=pltpu.MemorySpace.HBM),
        scratch_shapes=[
            pltpu.VMEM((224, 1024), jnp.bfloat16),
            pltpu.VMEM((1024, 1024), jnp.bfloat16),
            pltpu.VMEM((8, 224, 128), jnp.bfloat16),
            pltpu.SemaphoreType.DMA((2,)),
            pltpu.SemaphoreType.DMA((8,)),
            pltpu.SemaphoreType.DMA((4,)),
        ],
        compiler_params=pltpu.CompilerParams(vmem_limit_bytes=WHOLE_BYTES),
    )(grad_out, out_weight)


def pack_kernel(query_ref, key_ref, value_ref, filter_ref, partial_ref, send_ref, gated_ref):
    f32 = jnp.float32
    grad_gated = partial_ref[0].astype(f32)
    for j in range(1, 8):
        grad_gated = grad_gated + partial_ref[j].astype(f32)
    gated_ref[...] = grad_gated
    arrays = (
        key_ref[...].astype(f32) * value_ref[...].astype(f32),
        filter_ref[...],
        grad_gated * query_ref[...].astype(f32),
    )
    pad = jnp.zeros((16, 128), f32)
    for index, array in enumerate(arrays):
        for half in range(2):
            block = jnp.concatenate([array[112 * half:112 * half + 112], pad], axis=0).T
            for cc in range(4):
                row = (index * 2 + half) * 4 + cc
                send_ref[pl.ds(row, 32, stride=24), :] = block[32 * cc:32 * cc + 32]


def pack_call(query, key, value, filters, partials):
    return pl.pallas_call(
        pack_kernel,
        out_shape=(
            jax.ShapeDtypeStruct((768, 128), jnp.float32),
            jax.ShapeDtypeStruct((224, 128), jnp.float32),
        ),
        compiler_params=pltpu.CompilerParams(vmem_limit_bytes=VMEM_BYTES),
    )(query, key, value, filters, partials)


def conv_kernel(recv_ref, out_ref, xp, zp, fl, rh, rl, acc):
    f32, bf = jnp.float32, jnp.bfloat16
    row = lax.broadcasted_iota(jnp.int32, (16, 128), 0)
    lane = lax.broadcasted_iota(jnp.int32, (16, 128), 1)
    ri = lax.broadcasted_iota(jnp.int32, (64, 64), 0)
    ci = lax.broadcasted_iota(jnp.int32, (64, 64), 1)
    flip_blocks = jnp.where(ri + ci == 63, 1.0, 0.0).astype(bf)
    rows = lax.broadcasted_iota(jnp.int32, (128, 128), 0)
    cols = lax.broadcasted_iota(jnp.int32, (128, 128), 1)
    flip_lanes = jnp.where(rows + cols == 111, 1.0, 0.0).astype(bf)

    def split(block):
        high = block.astype(bf)
        return high, (block - high.astype(f32)).astype(bf)

    def flip(block):
        pair = jnp.concatenate(split(block), axis=0)
        turned = jnp.dot(pair, flip_lanes, preferred_element_type=f32).astype(bf)
        pair = jnp.concatenate([turned[0:64], turned[64:128]], axis=1)
        turned = jnp.dot(flip_blocks, pair, preferred_element_type=f32)
        return turned[:, 0:128] + turned[:, 128:256]

    xp[0:64, :] = jnp.zeros((64, 128), f32)
    zp[0:64, :] = jnp.zeros((64, 128), f32)
    for m in range(8):
        rh[128 * m + 112:128 * m + 128, :] = jnp.zeros((16, 1024), bf)
        rl[128 * m + 112:128 * m + 128, :] = jnp.zeros((16, 1024), bf)
    for d in range(2):
        acc[d, 0:8, :] = jnp.zeros((8, 1024), f32)
    fl[0:8, :] = jnp.zeros((8, 128), f32)

    for cc in range(4):
        for half in range(2):
            xp[pl.ds(64 + half, 32, stride=2), :] = recv_ref[pl.ds(half * 4 + cc, 32, stride=24), :]
            fl[pl.ds(8 + half, 32, stride=2), :] = recv_ref[pl.ds(8 + half * 4 + cc, 32, stride=24), :]
            zp[pl.ds(64 + half, 32, stride=2), :] = recv_ref[pl.ds(16 + half * 4 + cc, 32, stride=24), :]
        zp[64:128, :] = flip(zp[64:128, :])
        for k in range(64):
            m, r = k // 8, k % 8
            left = jnp.broadcast_to(fl[8 + k:9 + k, :], (16, 128))
            right = jnp.broadcast_to(pltpu.roll(fl[7 + k:8 + k, :], 16, 1), (16, 128))
            for p in range(7):
                src = jnp.where(lane < 128 - 16 * p - row, left, right)
                rolled = pltpu.roll(src, 16 * p, 1, stride=1, stride_axis=0)
                high, low = split(rolled)
                rh[128 * m + 16 * p:128 * m + 16 * p + 16, 128 * r:128 * r + 128] = high
                rl[128 * m + 16 * p:128 * m + 16 * p + 16, 128 * r:128 * r + 128] = low
        lhs = jnp.concatenate(
            [
                jnp.concatenate([ref[64 - 8 * m:128 - 8 * m, :] for m in range(8)], axis=1)
                for ref in (xp, zp)
            ],
            axis=0,
        )
        lhs_high, lhs_low = split(lhs)
        for n in range(0, 1024, 256):
            cols = slice(n, n + 256)
            prod = (
                jnp.dot(lhs_high, rh[:, cols], preferred_element_type=f32)
                + jnp.dot(lhs_low, rh[:, cols], preferred_element_type=f32)
                + jnp.dot(lhs_high, rl[:, cols], preferred_element_type=f32)
            )
            acc[0, 8:72, cols] = prod[0:64]
            acc[1, 8:72, cols] = prod[64:128]
        for d in range(2):
            total = acc[d, 8:72, 0:128]
            for r in range(1, 8):
                total = total + acc[d, 8 - r:72 - r, 128 * r:128 * r + 128]
            if d == 1:
                total = flip(total)
            xp[64:128, :] = total
            for half in range(2):
                out_ref[pl.ds((d * 2 + half) * 4 + cc, 32, stride=16), :] = xp[pl.ds(64 + half, 32, stride=2), :]

def conv_call(recv):
    f32, bf = jnp.float32, jnp.bfloat16
    return pl.pallas_call(
        conv_kernel,
        out_shape=jax.ShapeDtypeStruct((512, 128), f32),
        in_specs=[pl.BlockSpec(memory_space=pltpu.VMEM)],
        out_specs=pl.BlockSpec(memory_space=pltpu.VMEM),
        scratch_shapes=[
            pltpu.VMEM((128, 128), f32),
            pltpu.VMEM((128, 128), f32),
            pltpu.VMEM((72, 128), f32),
            pltpu.VMEM((1024, 1024), bf),
            pltpu.VMEM((1024, 1024), bf),
            pltpu.VMEM((2, 72, 1024), f32),
        ],
        compiler_params=pltpu.CompilerParams(vmem_limit_bytes=VMEM_BYTES),
    )(recv)


def unpack_kernel(
    recv_ref, query_ref, key_ref, value_ref, grad_ref, send_ref, gated_hbm, gq_ref, gk_ref, gv_ref,
    gated_ref, sem,
):
    f32 = jnp.float32
    pad = jnp.zeros((16, 128), f32)
    gated_copies = []
    for half in range(2):
        rows = slice(112 * half, 112 * half + 112)
        blocks = []
        for index in range(2):
            pieces = [recv_ref[pl.ds((index * 2 + half) * 4 + cc, 32, stride=16), :] for cc in range(4)]
            blocks.append(jnp.concatenate(pieces, axis=0))
        conv_out = blocks[0].T[0:112]
        grad_mixed = blocks[1].T[0:112]
        query = query_ref[rows, :].astype(f32)
        by_channel = jnp.concatenate([query, pad], axis=0).T * blocks[0]
        by_channel = by_channel.astype(jnp.bfloat16)
        for y in range(4):
            for j in range(8):
                send_ref[8 * y + j, 32 * half:32 * half + 32, :] = by_channel[32 * y:32 * y + 32]
        gated_ref[rows, :] = (query * conv_out).astype(jnp.bfloat16)
        gq_ref[rows, :] = grad_ref[rows, :] * conv_out
        gated_copy = pltpu.make_async_copy(
            gated_ref.at[pl.ds(112 * half, 112)], gated_hbm.at[pl.ds(112 * half, 112)], sem.at[half]
        )
        gated_copy.start()
        gated_copies.append(gated_copy)
        gk_ref[rows, :] = grad_mixed * value_ref[rows, :].astype(f32)
        gv_ref[rows, :] = grad_mixed * key_ref[rows, :].astype(f32)
    for gated_copy in gated_copies:
        gated_copy.wait()


def unpack_call(recv, query, key, value, grad_gated):
    bf = jnp.bfloat16
    grad = jax.ShapeDtypeStruct((224, 128), jnp.float32)
    return pl.pallas_call(
        unpack_kernel,
        out_shape=(
            jax.ShapeDtypeStruct((32, 64, 128), bf),
            jax.ShapeDtypeStruct((224, 128), bf),
            grad,
            grad,
            grad,
        ),
        out_specs=tuple(
            pl.BlockSpec(memory_space=pltpu.MemorySpace.HBM if index == 1 else pltpu.VMEM)
            for index in range(5)
        ),
        scratch_shapes=[
            pltpu.VMEM((224, 128), bf),
            pltpu.SemaphoreType.DMA((2,)),
        ],
        compiler_params=pltpu.CompilerParams(vmem_limit_bytes=VMEM_BYTES),
    )(recv, query, key, value, grad_gated)


def weight_kernel(own_ref, gated_ref, own, before, after, far_low, far_high, out_ref):
    parts = (
        (own, 0, 0, 0),
        (own, 112, 0, 1),
        (after, 0, 1, 0),
        (after, 112, 1, 1),
        (far_low, 0, 2, 0),
        (far_high, 0, 2, 1),
        (before, 0, 3, 0),
        (before, 112, 3, 1),
    )
    lhs = []
    for rows, start, turn, half in parts:
        block = gated_ref[pl.ds(8 * lax.rem(own_ref[0] + turn, 4), 8)]
        lhs.append(block[:, 32 * half:32 * half + 32, :].reshape(256, 128)[:, 0:112])
    for n in range(4):
        lanes = slice(256 * n, 256 * n + 256)
        total = None
        for gated, (rows, start, turn, half) in zip(lhs, parts):
            product = jnp.dot(
                gated, rows[start:start + 112, lanes], preferred_element_type=jnp.float32
            )
            total = product if total is None else total + product
        out_ref[:, lanes] = total.astype(jnp.bfloat16)


def weight_call(own_y, gathered, parts):
    vmem = pl.BlockSpec(memory_space=pltpu.VMEM)
    return pl.pallas_call(
        weight_kernel,
        out_shape=jax.ShapeDtypeStruct((256, 1024), jnp.bfloat16),
        in_specs=[pl.BlockSpec(memory_space=pltpu.SMEM)] + [vmem] * 6,
        out_specs=vmem,
        compiler_params=pltpu.CompilerParams(vmem_limit_bytes=VMEM_BYTES),
        cost_estimate=pl.CostEstimate(
            flops=2 * 256 * 896 * 1024, bytes_accessed=3 * 1024 * 1024, transcendentals=0
        ),
    )(own_y, gathered, *parts)


def layer_kernel(gated_ref, weight_ref, out_hbm, out_ref, sem):
    full = jnp.concatenate([gated_ref[j] for j in range(8)], axis=1)
    copies = []
    for n in range(4):
        cols = pl.ds(256 * n, 256)
        out_ref[:, 256 * n:256 * n + 256] = jnp.dot(
            full, weight_ref[:, 256 * n:256 * n + 256], preferred_element_type=jnp.float32
        )
        copies.append(pltpu.make_async_copy(out_ref.at[:, cols], out_hbm.at[:, cols], sem.at[n]))
        copies[-1].start()
    for copy in copies:
        copy.wait()


def layer_call(gathered, out_weight):
    vmem = pl.BlockSpec(memory_space=pltpu.VMEM)
    return pl.pallas_call(
        layer_kernel,
        out_shape=jax.ShapeDtypeStruct((224, 1024), jnp.float32),
        in_specs=[vmem, vmem],
        out_specs=pl.BlockSpec(memory_space=pltpu.MemorySpace.HBM),
        scratch_shapes=[
            pltpu.VMEM((224, 1024), jnp.float32),
            pltpu.SemaphoreType.DMA((4,)),
        ],
        compiler_params=pltpu.CompilerParams(vmem_limit_bytes=VMEM_BYTES),
    )(gathered, out_weight)


def local(query_slab, key_slab, value_slab, filters, out_weight, grad_out):
    up = [(4 * z + y, 4 * z + (y + 1) % 4) for z in range(8) for y in range(4)]
    down = [(4 * z + y, 4 * z + (y + 3) % 4) for z in range(8) for y in range(4)]
    along_z = [[4 * z + y for z in range(8)] for y in range(4)]
    planes = [list(range(32 * z, 32 * z + 32)) for z in range(8)]
    together = lax.optimization_barrier
    own_y = (lax.axis_index("ctx") % 4).astype(jnp.int32).reshape(1)
    partials = partial_call(grad_out, out_weight)
    own_grad, own_y, partials = together((grad_out, own_y, partials))
    partials = lax.all_to_all(partials, "chan", 0, 0)
    before = lax.ppermute(own_grad, "ctx", up)
    after = lax.ppermute(own_grad, "ctx", down)
    sent, grad_gated = pack_call(query_slab, key_slab, value_slab, filters, partials)
    before, after, sent = together((before, after, sent))
    by_channel = lax.all_to_all(sent.reshape(32, 24, 128), "ctx", 0, 0).reshape(768, 128)
    before, after, by_channel = together((before, after, by_channel))
    far_low = lax.ppermute(after[0:112], "ctx", down)
    far_high = lax.ppermute(before[112:224], "ctx", up)
    convolved = conv_call(by_channel)
    far_low, far_high, convolved = together((far_low, far_high, convolved))
    by_token = lax.all_to_all(convolved.reshape(32, 16, 128), "ctx", 0, 0).reshape(512, 128)
    plane_sent, gated, grad_query, grad_key, grad_value = unpack_call(
        by_token, query_slab, key_slab, value_slab, grad_gated
    )
    plane_gated = lax.all_to_all(plane_sent, ("ctx", "chan"), 0, 0, axis_index_groups=planes)
    weight_part = weight_call(
        own_y, plane_gated, (grad_out, before, after, far_low, far_high)
    ).reshape(8, 32, 1024)
    arrived = lax.all_to_all(weight_part, "ctx", 0, 0, axis_index_groups=along_z)
    full_gated = lax.all_gather(gated, "chan", axis=0)
    layer_out = layer_call(full_gated, out_weight)
    grad_weight = jnp.sum(arrived.astype(jnp.float32), axis=0)
    return (layer_out, grad_query, grad_key, grad_value, grad_weight)


def solution(mesh):
    placed = (
        P("ctx", "chan"),
        P("ctx", "chan"),
        P("ctx", "chan"),
        P("ctx", "chan"),
        P(None, "chan"),
        P("ctx", "chan"),
    )
    return jax.shard_map(
        local,
        mesh=mesh,
        in_specs=placed,
        out_specs=(
            P("ctx", "chan"),
            P("ctx", "chan"),
            P("ctx", "chan"),
            P("ctx", "chan"),
            P("ctx", "chan"),
        ),
        check_vma=False,
    )
```

```python
import jax
import jax.numpy as jnp
from jax import lax
from jax.experimental import pallas as pl
from jax.experimental.pallas import tpu as pltpu
from jax.sharding import PartitionSpec as P

VMEM_BYTES = 16 * 1024 * 1024
WHOLE_BYTES = 60 * 1024 * 1024


def partial_kernel(
    grad_hbm, weight_hbm, out_hbm, grad_ref, weight_ref, out_ref, grad_sem, weight_sem, out_sem
):
    def grad_copy(part):
        rows = pl.ds(112 * part, 112)
        return pltpu.make_async_copy(grad_hbm.at[rows], grad_ref.at[rows], grad_sem.at[part])

    def weight_copy(part):
        rows = pl.ds(128 * part, 128)
        return pltpu.make_async_copy(weight_hbm.at[rows], weight_ref.at[rows], weight_sem.at[part])

    for part in range(2):
        grad_copy(part).start()
    for part in range(8):
        weight_copy(part).start()
    for part in range(2):
        grad_copy(part).wait()
    out_copies = []
    for j in range(0, 8, 2):
        weight_copy(j).wait()
        weight_copy(j + 1).wait()
        product = lax.dot_general(
            grad_ref[...],
            weight_ref[128 * j:128 * j + 256, :],
            (((1,), (1,)), ((), ())),
            preferred_element_type=jnp.float32,
        ).astype(jnp.bfloat16)
        out_ref[j] = product[:, 0:128]
        out_ref[j + 1] = product[:, 128:256]
        out_copies.append(
            pltpu.make_async_copy(
                out_ref.at[pl.ds(j, 2)], out_hbm.at[pl.ds(j, 2)], out_sem.at[j // 2]
            )
        )
        out_copies[-1].start()
    for copy in out_copies:
        copy.wait()


def partial_call(grad_out, out_weight):
    return pl.pallas_call(
        partial_kernel,
        out_shape=jax.ShapeDtypeStruct((8, 224, 128), jnp.bfloat16),
        in_specs=[
            pl.BlockSpec(memory_space=pltpu.MemorySpace.HBM),
            pl.BlockSpec(memory_space=pltpu.MemorySpace.HBM),
        ],
        out_specs=pl.BlockSpec(memory_space=pltpu.MemorySpace.HBM),
        scratch_shapes=[
            pltpu.VMEM((224, 1024), jnp.bfloat16),
            pltpu.VMEM((1024, 1024), jnp.bfloat16),
            pltpu.VMEM((8, 224, 128), jnp.bfloat16),
            pltpu.SemaphoreType.DMA((2,)),
            pltpu.SemaphoreType.DMA((8,)),
            pltpu.SemaphoreType.DMA((4,)),
        ],
        compiler_params=pltpu.CompilerParams(vmem_limit_bytes=WHOLE_BYTES),
    )(grad_out, out_weight)


def pack_kernel(query_ref, key_ref, value_ref, filter_ref, partial_ref, send_ref, gated_ref, s1):
    f32 = jnp.float32
    grad_gated = partial_ref[0].astype(f32)
    for j in range(1, 8):
        grad_gated = grad_gated + partial_ref[j].astype(f32)
    gated_ref[...] = grad_gated
    mixed = key_ref[...].astype(f32) * value_ref[...].astype(f32)
    pieces = []
    for array in (mixed, filter_ref[...]):
        high = array.astype(jnp.bfloat16).astype(f32)
        pieces += [high, array - high]
    pieces.append(grad_gated * query_ref[...].astype(f32))
    pad = jnp.zeros((16, 128), f32)
    for index, array in enumerate(pieces):
        for half in range(2):
            block = jnp.concatenate([array[112 * half:112 * half + 112], pad], axis=0).T
            for cc in range(4):
                row = (index * 2 + half) * 4 + cc
                s1[pl.ds(row, 32, stride=40), :] = block[32 * cc:32 * cc + 32]
    send_ref[...] = s1[...].astype(jnp.bfloat16)


def pack_call(query, key, value, filters, partials):
    return pl.pallas_call(
        pack_kernel,
        out_shape=(
            jax.ShapeDtypeStruct((1280, 128), jnp.bfloat16),
            jax.ShapeDtypeStruct((224, 128), jnp.float32),
        ),
        scratch_shapes=[pltpu.VMEM((1280, 128), jnp.float32)],
        compiler_params=pltpu.CompilerParams(vmem_limit_bytes=VMEM_BYTES),
    )(query, key, value, filters, partials)


def conv_kernel(recv_ref, out_ref, s1, xp, zp, fl, rh, rl, acc):
    f32, bf = jnp.float32, jnp.bfloat16
    s1[...] = recv_ref[...].astype(f32)

    def piece(index, half, cc):
        return s1[pl.ds((index * 2 + half) * 4 + cc, 32, stride=40), :]

    row = lax.broadcasted_iota(jnp.int32, (16, 128), 0)
    lane = lax.broadcasted_iota(jnp.int32, (16, 128), 1)
    ri = lax.broadcasted_iota(jnp.int32, (64, 64), 0)
    ci = lax.broadcasted_iota(jnp.int32, (64, 64), 1)
    flip_blocks = jnp.where(ri + ci == 63, 1.0, 0.0).astype(bf)
    rows = lax.broadcasted_iota(jnp.int32, (128, 128), 0)
    cols = lax.broadcasted_iota(jnp.int32, (128, 128), 1)
    flip_lanes = jnp.where(rows + cols == 111, 1.0, 0.0).astype(bf)

    def split(block):
        high = block.astype(bf)
        return high, (block - high.astype(f32)).astype(bf)

    def flip(block):
        pair = jnp.concatenate(split(block), axis=0)
        turned = jnp.dot(pair, flip_lanes, preferred_element_type=f32).astype(bf)
        pair = jnp.concatenate([turned[0:64], turned[64:128]], axis=1)
        turned = jnp.dot(flip_blocks, pair, preferred_element_type=f32)
        return turned[:, 0:128] + turned[:, 128:256]

    xp[0:64, :] = jnp.zeros((64, 128), f32)
    zp[0:64, :] = jnp.zeros((64, 128), f32)
    for m in range(8):
        rh[128 * m + 112:128 * m + 128, :] = jnp.zeros((16, 1024), bf)
        rl[128 * m + 112:128 * m + 128, :] = jnp.zeros((16, 1024), bf)
    for d in range(2):
        acc[d, 0:8, :] = jnp.zeros((8, 1024), f32)
    fl[0:8, :] = jnp.zeros((8, 128), f32)

    for cc in range(4):
        for half in range(2):
            xp[pl.ds(64 + half, 32, stride=2), :] = piece(0, half, cc) + piece(1, half, cc)
            fl[pl.ds(8 + half, 32, stride=2), :] = piece(2, half, cc) + piece(3, half, cc)
            zp[pl.ds(64 + half, 32, stride=2), :] = piece(4, half, cc)
        zp[64:128, :] = flip(zp[64:128, :])
        for k in range(64):
            m, r = k // 8, k % 8
            left = jnp.broadcast_to(fl[8 + k:9 + k, :], (16, 128))
            right = jnp.broadcast_to(pltpu.roll(fl[7 + k:8 + k, :], 16, 1), (16, 128))
            for p in range(7):
                src = jnp.where(lane < 128 - 16 * p - row, left, right)
                rolled = pltpu.roll(src, 16 * p, 1, stride=1, stride_axis=0)
                high, low = split(rolled)
                rh[128 * m + 16 * p:128 * m + 16 * p + 16, 128 * r:128 * r + 128] = high
                rl[128 * m + 16 * p:128 * m + 16 * p + 16, 128 * r:128 * r + 128] = low
        lhs = jnp.concatenate(
            [
                jnp.concatenate([ref[64 - 8 * m:128 - 8 * m, :] for m in range(8)], axis=1)
                for ref in (xp, zp)
            ],
            axis=0,
        )
        lhs_high, lhs_low = split(lhs)
        for n in range(0, 1024, 256):
            cols = slice(n, n + 256)
            prod = (
                jnp.dot(lhs_high, rh[:, cols], preferred_element_type=f32)
                + jnp.dot(lhs_low, rh[:, cols], preferred_element_type=f32)
                + jnp.dot(lhs_high, rl[:, cols], preferred_element_type=f32)
            )
            acc[0, 8:72, cols] = prod[0:64]
            acc[1, 8:72, cols] = prod[64:128]
        for d in range(2):
            total = acc[d, 8:72, 0:128]
            for r in range(1, 8):
                total = total + acc[d, 8 - r:72 - r, 128 * r:128 * r + 128]
            if d == 1:
                total = flip(total)
            xp[64:128, :] = total
            for half in range(2):
                out_ref[pl.ds((d * 2 + half) * 4 + cc, 32, stride=16), :] = xp[pl.ds(64 + half, 32, stride=2), :]

def conv_call(recv):
    f32, bf = jnp.float32, jnp.bfloat16
    return pl.pallas_call(
        conv_kernel,
        out_shape=jax.ShapeDtypeStruct((512, 128), f32),
        in_specs=[pl.BlockSpec(memory_space=pltpu.VMEM)],
        out_specs=pl.BlockSpec(memory_space=pltpu.VMEM),
        scratch_shapes=[
            pltpu.VMEM((1280, 128), f32),
            pltpu.VMEM((128, 128), f32),
            pltpu.VMEM((128, 128), f32),
            pltpu.VMEM((72, 128), f32),
            pltpu.VMEM((1024, 1024), bf),
            pltpu.VMEM((1024, 1024), bf),
            pltpu.VMEM((2, 72, 1024), f32),
        ],
        compiler_params=pltpu.CompilerParams(vmem_limit_bytes=VMEM_BYTES),
    )(recv)


def unpack_kernel(
    recv_ref, query_ref, key_ref, value_ref, grad_ref, send_ref, gated_hbm, gq_ref, gk_ref, gv_ref,
    gated_ref, sem,
):
    f32 = jnp.float32
    pad = jnp.zeros((16, 128), f32)
    gated_copies = []
    for half in range(2):
        rows = slice(112 * half, 112 * half + 112)
        blocks = []
        for index in range(2):
            pieces = [recv_ref[pl.ds((index * 2 + half) * 4 + cc, 32, stride=16), :] for cc in range(4)]
            blocks.append(jnp.concatenate(pieces, axis=0))
        conv_out = blocks[0].T[0:112]
        grad_mixed = blocks[1].T[0:112]
        query = query_ref[rows, :].astype(f32)
        by_channel = jnp.concatenate([query, pad], axis=0).T * blocks[0]
        by_channel = by_channel.astype(jnp.bfloat16)
        for y in range(4):
            for j in range(8):
                send_ref[8 * y + j, 32 * half:32 * half + 32, :] = by_channel[32 * y:32 * y + 32]
        gated_ref[rows, :] = (query * conv_out).astype(jnp.bfloat16)
        gq_ref[rows, :] = grad_ref[rows, :] * conv_out
        gated_copy = pltpu.make_async_copy(
            gated_ref.at[pl.ds(112 * half, 112)], gated_hbm.at[pl.ds(112 * half, 112)], sem.at[half]
        )
        gated_copy.start()
        gated_copies.append(gated_copy)
        gk_ref[rows, :] = grad_mixed * value_ref[rows, :].astype(f32)
        gv_ref[rows, :] = grad_mixed * key_ref[rows, :].astype(f32)
    for gated_copy in gated_copies:
        gated_copy.wait()


def unpack_call(recv, query, key, value, grad_gated):
    bf = jnp.bfloat16
    grad = jax.ShapeDtypeStruct((224, 128), jnp.float32)
    return pl.pallas_call(
        unpack_kernel,
        out_shape=(
            jax.ShapeDtypeStruct((32, 64, 128), bf),
            jax.ShapeDtypeStruct((224, 128), bf),
            grad,
            grad,
            grad,
        ),
        out_specs=tuple(
            pl.BlockSpec(memory_space=pltpu.MemorySpace.HBM if index == 1 else pltpu.VMEM)
            for index in range(5)
        ),
        scratch_shapes=[
            pltpu.VMEM((224, 128), bf),
            pltpu.SemaphoreType.DMA((2,)),
        ],
        compiler_params=pltpu.CompilerParams(vmem_limit_bytes=VMEM_BYTES),
    )(recv, query, key, value, grad_gated)


def weight_kernel(own_ref, gated_ref, own, before, after, far_low, far_high, out_hbm, out_ref, sem):
    parts = (
        (own, 0, 0, 0),
        (own, 112, 0, 1),
        (after, 0, 1, 0),
        (after, 112, 1, 1),
        (far_low, 0, 2, 0),
        (far_high, 0, 2, 1),
        (before, 0, 3, 0),
        (before, 112, 3, 1),
    )
    lhs = []
    for rows, start, turn, half in parts:
        plane = 8 * lax.rem(own_ref[0] + turn, 4)
        blocks = [gated_ref[plane + j][32 * half:32 * half + 32, :] for j in range(8)]
        lhs.append(jnp.concatenate(blocks, axis=0)[:, 0:112])
    copies = []
    for n in range(4):
        cols = pl.ds(256 * n, 256)
        lanes = slice(256 * n, 256 * n + 256)
        total = None
        for gated, (rows, start, turn, half) in zip(lhs, parts):
            product = jnp.dot(
                gated, rows[start:start + 112, lanes], preferred_element_type=jnp.float32
            )
            total = product if total is None else total + product
        out_ref[:, lanes] = total.astype(jnp.bfloat16)
        copies.append(pltpu.make_async_copy(out_ref.at[:, cols], out_hbm.at[:, cols], sem.at[n]))
        copies[-1].start()
    for copy in copies:
        copy.wait()


def weight_call(own_y, gathered, parts):
    vmem = pl.BlockSpec(memory_space=pltpu.VMEM)
    return pl.pallas_call(
        weight_kernel,
        out_shape=jax.ShapeDtypeStruct((256, 1024), jnp.bfloat16),
        in_specs=[pl.BlockSpec(memory_space=pltpu.SMEM)] + [vmem] * 6,
        out_specs=pl.BlockSpec(memory_space=pltpu.MemorySpace.HBM),
        scratch_shapes=[
            pltpu.VMEM((256, 1024), jnp.bfloat16),
            pltpu.SemaphoreType.DMA((4,)),
        ],
        compiler_params=pltpu.CompilerParams(vmem_limit_bytes=VMEM_BYTES),
        cost_estimate=pl.CostEstimate(
            flops=2 * 256 * 896 * 1024, bytes_accessed=3 * 1024 * 1024, transcendentals=0
        ),
    )(own_y, gathered, *parts)


def layer_kernel(own_ref, pair_0, pair_1, pair_2, pair_3, weight_ref, out_hbm, out_ref, sem):
    chip, core = lax.div(own_ref[0], 2), lax.rem(own_ref[0], 2)
    blocks, starts = [], []
    for turn, pair in enumerate((pair_0, pair_1, pair_2, pair_3)):
        base = 256 * lax.rem(chip + turn, 4)
        for side in range(2):
            blocks.append(pair[side])
            starts.append(pl.multiple_of(base + 128 * lax.rem(core + side, 2), 128))
    full = jnp.concatenate(blocks, axis=1)
    copies = []
    for n in range(4):
        cols = pl.ds(256 * n, 256)
        lanes = slice(256 * n, 256 * n + 256)
        weight = jnp.concatenate([weight_ref[pl.ds(start, 128), lanes] for start in starts], axis=0)
        out_ref[:, lanes] = jnp.dot(full, weight, preferred_element_type=jnp.float32)
        copies.append(pltpu.make_async_copy(out_ref.at[:, cols], out_hbm.at[:, cols], sem.at[n]))
        copies[-1].start()
    for copy in copies:
        copy.wait()


def layer_call(own_chan, pairs, out_weight):
    vmem = pl.BlockSpec(memory_space=pltpu.VMEM)
    return pl.pallas_call(
        layer_kernel,
        out_shape=jax.ShapeDtypeStruct((224, 1024), jnp.float32),
        in_specs=[pl.BlockSpec(memory_space=pltpu.SMEM)] + [vmem] * 5,
        out_specs=pl.BlockSpec(memory_space=pltpu.MemorySpace.HBM),
        scratch_shapes=[
            pltpu.VMEM((224, 1024), jnp.float32),
            pltpu.SemaphoreType.DMA((4,)),
        ],
        compiler_params=pltpu.CompilerParams(vmem_limit_bytes=VMEM_BYTES),
    )(own_chan, *pairs, out_weight)


def local(query_slab, key_slab, value_slab, filters, out_weight, grad_out):
    up = [(4 * z + y, 4 * z + (y + 1) % 4) for z in range(8) for y in range(4)]
    down = [(4 * z + y, 4 * z + (y + 3) % 4) for z in range(8) for y in range(4)]
    along_z = [[4 * z + y for z in range(8)] for y in range(4)]
    planes = [list(range(32 * z, 32 * z + 32)) for z in range(8)]
    together = lax.optimization_barrier
    own_y = (lax.axis_index("ctx") % 4).astype(jnp.int32).reshape(1)
    partials = partial_call(grad_out, out_weight)
    own_chan = lax.axis_index("chan").astype(jnp.int32).reshape(1)
    own_grad, own_y, own_chan, partials = together((grad_out, own_y, own_chan, partials))
    partials = lax.all_to_all(partials, "chan", 0, 0)
    before = lax.ppermute(own_grad, "ctx", up)
    after = lax.ppermute(own_grad, "ctx", down)
    sent, grad_gated = pack_call(query_slab, key_slab, value_slab, filters, partials)
    before, after, sent = together((before, after, sent))
    by_channel = lax.all_to_all(sent.reshape(32, 40, 128), "ctx", 0, 0).reshape(1280, 128)
    before, after, by_channel = together((before, after, by_channel))
    far_low = lax.ppermute(after[0:112], "ctx", down)
    far_high = lax.ppermute(before[112:224], "ctx", up)
    convolved = conv_call(by_channel)
    far_low, far_high, convolved = together((far_low, far_high, convolved))
    by_token = lax.all_to_all(convolved.reshape(32, 16, 128), "ctx", 0, 0).reshape(512, 128)
    plane_sent, gated, grad_query, grad_key, grad_value = unpack_call(
        by_token, query_slab, key_slab, value_slab, grad_gated
    )
    plane_gated = lax.all_to_all(plane_sent, ("ctx", "chan"), 0, 0, axis_index_groups=planes)
    weight_part = weight_call(
        own_y, plane_gated, (grad_out, before, after, far_low, far_high)
    ).reshape(8, 32, 1024)
    gated, weight_part = together((gated, weight_part))
    arrived = lax.all_to_all(weight_part, "ctx", 0, 0, axis_index_groups=along_z)
    other = lax.ppermute(gated, "chan", [(i, i ^ 1) for i in range(8)])
    pair = jnp.stack([gated, other])
    pairs = [pair]
    for turn in range(1, 4):
        route = [((i + 2 * turn) % 8, i) for i in range(8)]
        pairs.append(lax.ppermute(pair, "chan", route))
    layer_out = layer_call(own_chan, pairs, out_weight)
    grad_weight = jnp.sum(arrived.astype(jnp.float32), axis=0)
    return (layer_out, grad_query, grad_key, grad_value, grad_weight)


def solution(mesh):
    placed = (
        P("ctx", "chan"),
        P("ctx", "chan"),
        P("ctx", "chan"),
        P("ctx", "chan"),
        P(None, "chan"),
        P("ctx", "chan"),
    )
    return jax.shard_map(
        local,
        mesh=mesh,
        in_specs=placed,
        out_specs=(
            P("ctx", "chan"),
            P("ctx", "chan"),
            P("ctx", "chan"),
            P("ctx", "chan"),
            P("ctx", "chan"),
        ),
        check_vma=False,
    )
```

```python
import jax
import jax.numpy as jnp
from jax import lax
from jax.experimental import pallas as pl
from jax.experimental.pallas import tpu as pltpu
from jax.sharding import PartitionSpec as P

VMEM_BYTES = 16 * 1024 * 1024
WHOLE_BYTES = 60 * 1024 * 1024


def partial_kernel(
    grad_hbm, weight_hbm, out_hbm, grad_ref, weight_ref, out_ref, grad_sem, weight_sem, out_sem
):
    def grad_copy(part):
        rows = pl.ds(112 * part, 112)
        return pltpu.make_async_copy(grad_hbm.at[rows], grad_ref.at[rows], grad_sem.at[part])

    def weight_copy(part):
        rows = pl.ds(128 * part, 128)
        return pltpu.make_async_copy(weight_hbm.at[rows], weight_ref.at[rows], weight_sem.at[part])

    for part in range(2):
        grad_copy(part).start()
    for part in range(8):
        weight_copy(part).start()
    for part in range(2):
        grad_copy(part).wait()
    out_copies = []
    for j in range(0, 8, 2):
        weight_copy(j).wait()
        weight_copy(j + 1).wait()
        product = lax.dot_general(
            grad_ref[...],
            weight_ref[128 * j:128 * j + 256, :],
            (((1,), (1,)), ((), ())),
            preferred_element_type=jnp.float32,
        ).astype(jnp.bfloat16)
        out_ref[j] = product[:, 0:128]
        out_ref[j + 1] = product[:, 128:256]
        out_copies.append(
            pltpu.make_async_copy(
                out_ref.at[pl.ds(j, 2)], out_hbm.at[pl.ds(j, 2)], out_sem.at[j // 2]
            )
        )
        out_copies[-1].start()
    for copy in out_copies:
        copy.wait()


def partial_call(grad_out, out_weight):
    return pl.pallas_call(
        partial_kernel,
        out_shape=jax.ShapeDtypeStruct((8, 224, 128), jnp.bfloat16),
        in_specs=[
            pl.BlockSpec(memory_space=pltpu.MemorySpace.HBM),
            pl.BlockSpec(memory_space=pltpu.MemorySpace.HBM),
        ],
        out_specs=pl.BlockSpec(memory_space=pltpu.MemorySpace.HBM),
        scratch_shapes=[
            pltpu.VMEM((224, 1024), jnp.bfloat16),
            pltpu.VMEM((1024, 1024), jnp.bfloat16),
            pltpu.VMEM((8, 224, 128), jnp.bfloat16),
            pltpu.SemaphoreType.DMA((2,)),
            pltpu.SemaphoreType.DMA((8,)),
            pltpu.SemaphoreType.DMA((4,)),
        ],
        compiler_params=pltpu.CompilerParams(vmem_limit_bytes=WHOLE_BYTES),
    )(grad_out, out_weight)


def pack_kernel(query_ref, key_ref, value_ref, filter_ref, partial_ref, send_ref, gated_ref, s1):
    f32 = jnp.float32
    grad_gated = partial_ref[0].astype(f32)
    for j in range(1, 8):
        grad_gated = grad_gated + partial_ref[j].astype(f32)
    gated_ref[...] = grad_gated
    mixed = key_ref[...].astype(f32) * value_ref[...].astype(f32)
    pieces = []
    for array in (mixed, filter_ref[...]):
        high = array.astype(jnp.bfloat16).astype(f32)
        pieces += [high, array - high]
    pieces.append(grad_gated * query_ref[...].astype(f32))
    pad = jnp.zeros((16, 128), f32)
    for index, array in enumerate(pieces):
        for half in range(2):
            block = jnp.concatenate([array[112 * half:112 * half + 112], pad], axis=0).T
            for cc in range(4):
                row = (index * 2 + half) * 4 + cc
                s1[pl.ds(row, 32, stride=40), :] = block[32 * cc:32 * cc + 32]
    send_ref[...] = s1[...].astype(jnp.bfloat16)


def pack_call(query, key, value, filters, partials):
    return pl.pallas_call(
        pack_kernel,
        out_shape=(
            jax.ShapeDtypeStruct((1280, 128), jnp.bfloat16),
            jax.ShapeDtypeStruct((224, 128), jnp.float32),
        ),
        scratch_shapes=[pltpu.VMEM((1280, 128), jnp.float32)],
        compiler_params=pltpu.CompilerParams(vmem_limit_bytes=VMEM_BYTES),
    )(query, key, value, filters, partials)


def conv_kernel(recv_ref, out_ref, s1, xp, zp, fl, rh, rl, acc):
    f32, bf = jnp.float32, jnp.bfloat16
    s1[...] = recv_ref[...].astype(f32)

    def piece(index, half, cc):
        return s1[pl.ds((index * 2 + half) * 4 + cc, 32, stride=40), :]

    row = lax.broadcasted_iota(jnp.int32, (16, 128), 0)
    lane = lax.broadcasted_iota(jnp.int32, (16, 128), 1)
    ri = lax.broadcasted_iota(jnp.int32, (64, 64), 0)
    ci = lax.broadcasted_iota(jnp.int32, (64, 64), 1)
    flip_blocks = jnp.where(ri + ci == 63, 1.0, 0.0).astype(bf)
    rows = lax.broadcasted_iota(jnp.int32, (128, 128), 0)
    cols = lax.broadcasted_iota(jnp.int32, (128, 128), 1)
    flip_lanes = jnp.where(rows + cols == 111, 1.0, 0.0).astype(bf)

    def split(block):
        high = block.astype(bf)
        return high, (block - high.astype(f32)).astype(bf)

    def flip(block):
        pair = jnp.concatenate(split(block), axis=0)
        turned = jnp.dot(pair, flip_lanes, preferred_element_type=f32).astype(bf)
        pair = jnp.concatenate([turned[0:64], turned[64:128]], axis=1)
        turned = jnp.dot(flip_blocks, pair, preferred_element_type=f32)
        return turned[:, 0:128] + turned[:, 128:256]

    xp[0:64, :] = jnp.zeros((64, 128), f32)
    zp[0:64, :] = jnp.zeros((64, 128), f32)
    for m in range(8):
        rh[128 * m + 112:128 * m + 128, :] = jnp.zeros((16, 1024), bf)
        rl[128 * m + 112:128 * m + 128, :] = jnp.zeros((16, 1024), bf)
    for d in range(2):
        acc[d, 0:8, :] = jnp.zeros((8, 1024), f32)
    fl[0:8, :] = jnp.zeros((8, 128), f32)

    for cc in range(4):
        for half in range(2):
            xp[pl.ds(64 + half, 32, stride=2), :] = piece(0, half, cc) + piece(1, half, cc)
            fl[pl.ds(8 + half, 32, stride=2), :] = piece(2, half, cc) + piece(3, half, cc)
            zp[pl.ds(64 + half, 32, stride=2), :] = piece(4, half, cc)
        zp[64:128, :] = flip(zp[64:128, :])
        for k in range(64):
            m, r = k // 8, k % 8
            left = jnp.broadcast_to(fl[8 + k:9 + k, :], (16, 128))
            right = jnp.broadcast_to(pltpu.roll(fl[7 + k:8 + k, :], 16, 1), (16, 128))
            for p in range(7):
                src = jnp.where(lane < 128 - 16 * p - row, left, right)
                rolled = pltpu.roll(src, 16 * p, 1, stride=1, stride_axis=0)
                high, low = split(rolled)
                rh[128 * m + 16 * p:128 * m + 16 * p + 16, 128 * r:128 * r + 128] = high
                rl[128 * m + 16 * p:128 * m + 16 * p + 16, 128 * r:128 * r + 128] = low
        lhs = jnp.concatenate(
            [
                jnp.concatenate([ref[64 - 8 * m:128 - 8 * m, :] for m in range(8)], axis=1)
                for ref in (xp, zp)
            ],
            axis=0,
        )
        lhs_high, lhs_low = split(lhs)
        for n in range(0, 1024, 256):
            cols = slice(n, n + 256)
            prod = (
                jnp.dot(lhs_high, rh[:, cols], preferred_element_type=f32)
                + jnp.dot(lhs_low, rh[:, cols], preferred_element_type=f32)
                + jnp.dot(lhs_high, rl[:, cols], preferred_element_type=f32)
            )
            acc[0, 8:72, cols] = prod[0:64]
            acc[1, 8:72, cols] = prod[64:128]
        for d in range(2):
            total = acc[d, 8:72, 0:128]
            for r in range(1, 8):
                total = total + acc[d, 8 - r:72 - r, 128 * r:128 * r + 128]
            if d == 1:
                total = flip(total)
            xp[64:128, :] = total
            for half in range(2):
                out_ref[pl.ds((d * 2 + half) * 4 + cc, 32, stride=16), :] = xp[pl.ds(64 + half, 32, stride=2), :]

def conv_call(recv):
    f32, bf = jnp.float32, jnp.bfloat16
    return pl.pallas_call(
        conv_kernel,
        out_shape=jax.ShapeDtypeStruct((512, 128), f32),
        in_specs=[pl.BlockSpec(memory_space=pltpu.VMEM)],
        out_specs=pl.BlockSpec(memory_space=pltpu.VMEM),
        scratch_shapes=[
            pltpu.VMEM((1280, 128), f32),
            pltpu.VMEM((128, 128), f32),
            pltpu.VMEM((128, 128), f32),
            pltpu.VMEM((72, 128), f32),
            pltpu.VMEM((1024, 1024), bf),
            pltpu.VMEM((1024, 1024), bf),
            pltpu.VMEM((2, 72, 1024), f32),
        ],
        compiler_params=pltpu.CompilerParams(vmem_limit_bytes=VMEM_BYTES),
    )(recv)


def by_token_block(recv_ref, index, half):
    pieces = [recv_ref[pl.ds((index * 2 + half) * 4 + cc, 32, stride=16), :] for cc in range(4)]
    return jnp.concatenate(pieces, axis=0)


def gate_kernel(recv_ref, query_ref, send_ref, gated_ref, conv_ref):
    f32 = jnp.float32
    pad = jnp.zeros((16, 128), f32)
    for half in range(2):
        rows = slice(112 * half, 112 * half + 112)
        block = by_token_block(recv_ref, 0, half)
        query = query_ref[rows, :].astype(f32)
        by_channel = jnp.concatenate([query, pad], axis=0).T * block
        by_channel = by_channel.astype(jnp.bfloat16)
        for y in range(4):
            for j in range(8):
                send_ref[8 * y + j, 32 * half:32 * half + 32, :] = by_channel[32 * y:32 * y + 32]
        conv_out = block.T[0:112]
        conv_ref[rows, :] = conv_out
        gated_ref[rows, :] = (query * conv_out).astype(jnp.bfloat16)


def gate_call(recv, query):
    bf = jnp.bfloat16
    return pl.pallas_call(
        gate_kernel,
        out_shape=(
            jax.ShapeDtypeStruct((32, 64, 128), bf),
            jax.ShapeDtypeStruct((224, 128), bf),
            jax.ShapeDtypeStruct((224, 128), jnp.float32),
        ),
        compiler_params=pltpu.CompilerParams(vmem_limit_bytes=VMEM_BYTES),
    )(recv, query)


def grads_kernel(recv_ref, conv_ref, key_ref, value_ref, grad_ref, gq_ref, gk_ref, gv_ref):
    f32 = jnp.float32
    gq_ref[...] = grad_ref[...] * conv_ref[...]
    for half in range(2):
        rows = slice(112 * half, 112 * half + 112)
        grad_mixed = by_token_block(recv_ref, 1, half).T[0:112]
        gk_ref[rows, :] = grad_mixed * value_ref[rows, :].astype(f32)
        gv_ref[rows, :] = grad_mixed * key_ref[rows, :].astype(f32)


def grads_call(recv, conv_out, key, value, grad_gated):
    return pl.pallas_call(
        grads_kernel,
        out_shape=(jax.ShapeDtypeStruct((224, 128), jnp.float32),) * 3,
        compiler_params=pltpu.CompilerParams(vmem_limit_bytes=4 * 1024 * 1024),
    )(recv, conv_out, key, value, grad_gated)


def sum_kernel(parts_ref, out_ref):
    total = parts_ref[0].astype(jnp.float32)
    for index in range(1, 8):
        total = total + parts_ref[index].astype(jnp.float32)
    out_ref[...] = total


def sum_call(parts):
    return pl.pallas_call(
        sum_kernel,
        out_shape=jax.ShapeDtypeStruct((32, 1024), jnp.float32),
        compiler_params=pltpu.CompilerParams(vmem_limit_bytes=4 * 1024 * 1024),
    )(parts)


def weight_kernel(own_ref, gated_ref, own, before, after, far_low, far_high, out_hbm, out_ref, sem):
    parts = (
        (own, 0, 0, 0),
        (own, 112, 0, 1),
        (after, 0, 1, 0),
        (after, 112, 1, 1),
        (far_low, 0, 2, 0),
        (far_high, 0, 2, 1),
        (before, 0, 3, 0),
        (before, 112, 3, 1),
    )
    lhs = []
    for rows, start, turn, half in parts:
        plane = 8 * lax.rem(own_ref[0] + turn, 4)
        blocks = [gated_ref[plane + j][32 * half:32 * half + 32, :] for j in range(8)]
        lhs.append(jnp.concatenate(blocks, axis=0)[:, 0:112])
    copies = []
    for n in range(4):
        cols = pl.ds(256 * n, 256)
        lanes = slice(256 * n, 256 * n + 256)
        total = None
        for gated, (rows, start, turn, half) in zip(lhs, parts):
            product = jnp.dot(
                gated, rows[start:start + 112, lanes], preferred_element_type=jnp.float32
            )
            total = product if total is None else total + product
        out_ref[:, lanes] = total.astype(jnp.bfloat16)
        copies.append(pltpu.make_async_copy(out_ref.at[:, cols], out_hbm.at[:, cols], sem.at[n]))
        copies[-1].start()
    for copy in copies:
        copy.wait()


def weight_call(own_y, gathered, parts):
    vmem = pl.BlockSpec(memory_space=pltpu.VMEM)
    return pl.pallas_call(
        weight_kernel,
        out_shape=jax.ShapeDtypeStruct((256, 1024), jnp.bfloat16),
        in_specs=[pl.BlockSpec(memory_space=pltpu.SMEM)] + [vmem] * 6,
        out_specs=pl.BlockSpec(memory_space=pltpu.MemorySpace.HBM),
        scratch_shapes=[
            pltpu.VMEM((256, 1024), jnp.bfloat16),
            pltpu.SemaphoreType.DMA((4,)),
        ],
        compiler_params=pltpu.CompilerParams(vmem_limit_bytes=VMEM_BYTES),
        cost_estimate=pl.CostEstimate(
            flops=2 * 256 * 896 * 1024, bytes_accessed=3 * 1024 * 1024, transcendentals=0
        ),
    )(own_y, gathered, *parts)


def layer_kernel(own_ref, pair_0, pair_1, pair_2, pair_3, weight_ref, out_hbm, out_ref, sem):
    chip, core = lax.div(own_ref[0], 2), lax.rem(own_ref[0], 2)
    blocks, starts = [], []
    for turn, pair in enumerate((pair_0, pair_1, pair_2, pair_3)):
        base = 256 * lax.rem(chip + turn, 4)
        for side in range(2):
            blocks.append(pair[side])
            starts.append(pl.multiple_of(base + 128 * lax.rem(core + side, 2), 128))
    full = jnp.concatenate(blocks, axis=1)
    copies = []
    for n in range(4):
        cols = pl.ds(256 * n, 256)
        lanes = slice(256 * n, 256 * n + 256)
        weight = jnp.concatenate([weight_ref[pl.ds(start, 128), lanes] for start in starts], axis=0)
        out_ref[:, lanes] = jnp.dot(full, weight, preferred_element_type=jnp.float32)
        copies.append(pltpu.make_async_copy(out_ref.at[:, cols], out_hbm.at[:, cols], sem.at[n]))
        copies[-1].start()
    for copy in copies:
        copy.wait()


def layer_call(own_chan, pairs, out_weight):
    vmem = pl.BlockSpec(memory_space=pltpu.VMEM)
    return pl.pallas_call(
        layer_kernel,
        out_shape=jax.ShapeDtypeStruct((224, 1024), jnp.float32),
        in_specs=[pl.BlockSpec(memory_space=pltpu.SMEM)] + [vmem] * 5,
        out_specs=pl.BlockSpec(memory_space=pltpu.MemorySpace.HBM),
        scratch_shapes=[
            pltpu.VMEM((224, 1024), jnp.float32),
            pltpu.SemaphoreType.DMA((4,)),
        ],
        compiler_params=pltpu.CompilerParams(vmem_limit_bytes=VMEM_BYTES),
    )(own_chan, *pairs, out_weight)


def local(query_slab, key_slab, value_slab, filters, out_weight, grad_out):
    up = [(4 * z + y, 4 * z + (y + 1) % 4) for z in range(8) for y in range(4)]
    down = [(4 * z + y, 4 * z + (y + 3) % 4) for z in range(8) for y in range(4)]
    along_z = [[4 * z + y for z in range(8)] for y in range(4)]
    planes = [list(range(32 * z, 32 * z + 32)) for z in range(8)]
    together = lax.optimization_barrier
    own_y = (lax.axis_index("ctx") % 4).astype(jnp.int32).reshape(1)
    partials = partial_call(grad_out, out_weight)
    own_chan = lax.axis_index("chan").astype(jnp.int32).reshape(1)
    own_grad, own_y, own_chan, partials = together((grad_out, own_y, own_chan, partials))
    partials = lax.all_to_all(partials, "chan", 0, 0)
    before = lax.ppermute(own_grad, "ctx", up)
    after = lax.ppermute(own_grad, "ctx", down)
    sent, grad_gated = pack_call(query_slab, key_slab, value_slab, filters, partials)
    before, after, sent = together((before, after, sent))
    by_channel = lax.all_to_all(sent.reshape(32, 40, 128), "ctx", 0, 0).reshape(1280, 128)
    before, after, by_channel = together((before, after, by_channel))
    far_low = lax.ppermute(after[0:112], "ctx", down)
    far_high = lax.ppermute(before[112:224], "ctx", up)
    convolved = conv_call(by_channel)
    far_low, far_high, convolved = together((far_low, far_high, convolved))
    by_token = lax.all_to_all(convolved.reshape(32, 16, 128), "ctx", 0, 0).reshape(512, 128)
    plane_sent, gated, conv_out = gate_call(by_token, query_slab)
    plane_gated = lax.all_to_all(plane_sent, ("ctx", "chan"), 0, 0, axis_index_groups=planes)
    weight_part = weight_call(
        own_y, plane_gated, (grad_out, before, after, far_low, far_high)
    ).reshape(8, 32, 1024)
    gated, conv_out, weight_part = together((gated, conv_out, weight_part))
    arrived = lax.all_to_all(weight_part, "ctx", 0, 0, axis_index_groups=along_z)
    other = lax.ppermute(gated, "chan", [(i, i ^ 1) for i in range(8)])
    pair = jnp.stack([gated, other])
    pairs = [pair]
    for turn in range(1, 4):
        route = [((i + 2 * turn) % 8, i) for i in range(8)]
        pairs.append(lax.ppermute(pair, "chan", route))
    layer_out = layer_call(own_chan, pairs, out_weight)
    grad_query, grad_key, grad_value = grads_call(
        by_token, conv_out, key_slab, value_slab, grad_gated
    )
    grad_weight = sum_call(arrived)
    return (layer_out, grad_query, grad_key, grad_value, grad_weight)


def solution(mesh):
    placed = (
        P("ctx", "chan"),
        P("ctx", "chan"),
        P("ctx", "chan"),
        P("ctx", "chan"),
        P(None, "chan"),
        P("ctx", "chan"),
    )
    return jax.shard_map(
        local,
        mesh=mesh,
        in_specs=placed,
        out_specs=(
            P("ctx", "chan"),
            P("ctx", "chan"),
            P("ctx", "chan"),
            P("ctx", "chan"),
            P("ctx", "chan"),
        ),
        check_vma=False,
    )
```
